512 devices in a mesh: mem: 8 (over x, core), col: 64 (over z, y).
Axes of the slice: x: 4, y: 8, z: 8, core: 2. Of those that a mesh axis runs over, the one named last changes fastest.
Arguments:
- ensemble: bfloat16 [80, 512, 1024], P('mem', 'col'), may hold values from -6 to 6
- obs_prior: float32 [80, 16384], P(None, 'col'), may hold values from -6 to 6
- obs_value: float32 [16384], P('col'), may hold values from -8 to 8
- obs_var: float32 [16384], P('col'), may hold values from 0.25 to 4
- obs_noise: float32 [80, 16384], P(None, 'col'), may hold values from -6 to 6
- obs_block: int32 [16384], P('col'), may hold values from 0 to 511
- batch_owner: int32 [8], replicated, may hold values from 0 to 63, as said below
Outputs:
- analysis: bfloat16 [80, 512, 1024], P('mem', 'col')
- obs_posterior: float32 [80, 16384], P(None, 'col')
The draws below stay inside these ranges and needn't reach their ends.
Inputs may be any that keep to these rules, and one draw needn't show every extreme that they name: `batch_owner`: the 8 entries are distinct; both 0 and 63 occur.
All inputs are finite; a program needn't handle non-finite values.
Results may differ from the reference program's by a relative error of at most 0.001.
Values may be sent and summed in bfloat16 or wider, within the bound.
A program may use at most 128 MiB of HBM per device.

```python
import math
import jax
import jax.numpy as jnp
from jax import lax

MEMBERS = 80
BATCH = 256
BATCHES = 8
CELLS = 1024
BLOCKS = 512
OBS = 16384


def draw_batch_owner(key, part):
    columns = OBS // BATCH
    opening, second = jax.random.split(key)
    interior = jax.random.permutation(opening, jnp.arange(1, columns - 1, dtype=jnp.int32))[:BATCHES - 2]
    owners_all = jnp.concatenate([interior, jnp.array([0, columns - 1], dtype=jnp.int32)])
    return jax.random.permutation(second, owners_all)


def touch_ends(values, stream_key, low, top_value):
    spot = [jax.random.randint(jax.random.fold_in(stream_key, axis), (), 0, length) for axis, length in enumerate(values.shape)]
    longest = values.shape.index(max(values.shape))
    next_to = spot[:longest] + [(spot[longest] + 1) % values.shape[longest]] + spot[longest + 1:]
    return values.at[tuple(spot)].set(low).at[tuple(next_to)].set(top_value)


def shard_levels(stream_key, dims, cuts, low, largest):
    def one(dim, shards_of):
        steps = jax.random.uniform(jax.random.fold_in(jax.random.fold_in(stream_key, 6), dim), (shards_of,), jnp.float32, low / len(cuts), largest / len(cuts))
        return jnp.repeat(jnp.exp(steps), dims[dim] // shards_of).reshape((-1,) + (1,) * (len(dims) - dim - 1))

    level = one(*cuts[0])
    for cut in cuts[1:]:
        level = level * one(*cut)
    return level


def gaussian(own_key, extent, deviation, most, cuts=(), kind=jnp.bfloat16):
    drawn = deviation * jax.random.normal(own_key, extent, jnp.float32)
    if cuts:
        drawn = drawn * shard_levels(own_key, extent, cuts, -0.22, 0.18)
    return jnp.clip(drawn, -most, most).astype(kind)


def setup_inputs(seed: int = 0) -> dict:
    streams_of = jax.random.split(jax.random.key(seed), 8)
    return {
        "ensemble": gaussian(streams_of[0], (MEMBERS, BLOCKS, CELLS), 1.0, 6.0, ((0, 8), (1, 64))),
        "obs_prior": gaussian(streams_of[1], (MEMBERS, OBS), 1.0, 6.0, ((1, 64),), jnp.float32),
        "obs_value": gaussian(streams_of[2], (OBS,), 1.5, 8.0, ((0, 64),), jnp.float32),
        "obs_var": jnp.clip(jnp.exp(math.log(4.0) - 2.7725887 * jax.random.uniform(streams_of[3], (OBS,), jnp.float32) ** shard_levels(streams_of[3], (OBS,), ((0, 64),), -0.2, 0.2)), 0.25, 4.0),
        "obs_noise": gaussian(streams_of[4], (MEMBERS, OBS), 1.0, 6.0, ((1, 64),), jnp.float32),
        "obs_block": touch_ends(jax.random.randint(streams_of[5], (OBS,), 0, BLOCKS), jax.random.fold_in(streams_of[5], 1), 0, BLOCKS - 1).astype(jnp.int32),
        "batch_owner": draw_batch_owner(jax.random.fold_in(streams_of[7], 71), 0),
    }


highest = lax.Precision.HIGHEST

def taper(offset, blocks):
    cosine = jnp.cos(offset * (math.pi / blocks))
    square = cosine * cosine
    fourth = square * square
    return fourth * fourth

def batch_factors(priors_now, perturbed, variance, position, blocks):
    members = priors_now.shape[0]
    spread = priors_now - lax.optimization_barrier(jnp.mean(priors_now, axis=0, keepdims=True))
    covariance = jnp.dot(spread.T.astype(jnp.float32), spread.astype(jnp.float32), precision=highest, preferred_element_type=jnp.float32) / (members - 1)
    system = taper(position[:, None] - position[None, :], blocks) * covariance + jnp.diag(variance)
    factor_low = jnp.linalg.cholesky(system)
    solved = jax.scipy.linalg.cho_solve((factor_low, True), (perturbed - priors_now).T)
    return (spread, solved)

def regress(values_in, spread, solved, weight):
    members = values_in.shape[0]
    anomaly = values_in - lax.optimization_barrier(jnp.mean(values_in, axis=0, keepdims=True))
    covariance = jnp.dot(spread.T.astype(jnp.float32), anomaly.astype(jnp.float32), precision=highest, preferred_element_type=jnp.float32) / (members - 1)
    return values_in + jnp.dot(solved.T.astype(jnp.float32), (weight * covariance).astype(jnp.float32), precision=highest, preferred_element_type=jnp.float32)

def reference(ensemble, obs_prior, obs_value, obs_var, obs_noise, obs_block, batch_owner):
    perturbed_all = obs_value[None, :] + jnp.sqrt(obs_var)[None, :] * obs_noise
    positions_all = obs_block.astype(jnp.float32)
    obs_pool = obs_prior
    factors = []
    for batch_number in range(BATCHES):
        start = (batch_owner[batch_number] * BATCH).astype(jnp.int32)
        priors_now = lax.dynamic_slice_in_dim(obs_pool, start, BATCH, 1)
        perturbed = lax.dynamic_slice_in_dim(perturbed_all, start, BATCH, 1)
        variance = lax.dynamic_slice_in_dim(obs_var, start, BATCH, 0)
        position = lax.dynamic_slice_in_dim(positions_all, start, BATCH, 0)
        spread, solved = batch_factors(priors_now, perturbed, variance, position, BLOCKS)
        obs_pool = regress(obs_pool, spread, solved, taper(position[:, None] - positions_all[None, :], BLOCKS))
        factors.append((spread, solved, position))

    def one_block(block_id):
        state_cols = lax.dynamic_index_in_dim(ensemble, block_id, 1, keepdims=False).astype(jnp.float32)
        block_pos = block_id.astype(jnp.float32)
        for spread, solved, position in factors:
            state_cols = regress(state_cols, spread, solved, taper(block_pos - position, BLOCKS)[:, None])
        return state_cols.astype(jnp.bfloat16)
    result = lax.map(one_block, jnp.arange(BLOCKS, dtype=jnp.int32))
    analysis = jnp.transpose(result, (1, 0, 2))
    return (analysis, obs_pool)
```

```python
import functools
import math

import jax
import jax.numpy as jnp
from jax import lax
from jax.experimental import pallas as pl
from jax.experimental.pallas import tpu as pltpu
from jax.sharding import PartitionSpec as P

MESH = pl.DeviceIdType.MESH
HIGHEST = lax.Precision.HIGHEST
MEMBERS = 80
BATCH = 256
HALF = 128
SLICE = 24
VAR_ROW, COS_ROW, SIN_ROW = 160, 161, 162


def dot(a, b, precision=HIGHEST):
    return jnp.dot(a, b, precision=precision, preferred_element_type=jnp.float32)


def eighth(x):
    x = x * x
    x = x * x
    return x * x


def exchange(own_ref, owner_ref, all_ref, along_y, picked, along_z, chosen, slots, sends, recvs):
    m = lax.axis_index("mem")
    c = lax.axis_index("col")
    x, core = m // 2, lax.rem(m, 2)
    z, y = c // 8, lax.rem(c, 8)
    sibling = x * 2 + 1 - core
    barrier = pltpu.get_barrier_semaphore()
    to_y = [(m, z * 8 + lax.rem(y + i, 8)) for i in range(1, 8)]
    to_z = [(m, lax.rem(z + i, 8) * 8 + y) for i in range(1, 8)]
    to_x = [(lax.rem(x + i, 4) * 2 + core, c) for i in range(1, 4)]
    for peer in to_y + to_z + to_x + [(sibling, c)]:
        pl.semaphore_signal(barrier, inc=1, device_id=peer, device_id_type=MESH)
    pl.semaphore_wait(barrier, 18)

    def copy(phase, i, src, dst, peer):
        return pltpu.make_async_remote_copy(
            src_ref=src,
            dst_ref=dst,
            send_sem=sends.at[phase, i],
            recv_sem=recvs.at[phase, i],
            device_id=peer,
            device_id_type=MESH,
        )

    def gather(phase, src, dst, mine, peers):
        for i, peer in enumerate(peers):
            copy(phase, i, src, dst.at[mine], peer).start()
        dst[mine] = src[...]
        n = len(peers) + 1
        for i, peer in enumerate(peers):
            one = copy(phase, i, src, dst.at[lax.rem(mine + n - 1 - i, n)], peer)
            one.wait_recv()
            one.wait_send()

    gather(0, own_ref, along_y, y, to_y)
    owner = owner_ref[y]
    picked[...] = along_y[lax.rem(owner, 8)]
    gather(1, picked, along_z, z, to_z)
    chosen[...] = along_z[owner // 8]
    gather(2, chosen, slots, y, to_y)
    there = (sibling, c)
    for i, peer in enumerate(to_x):
        copy(3, i, slots, all_ref.at[m], peer).start()
    copy(4, 0, slots, all_ref.at[m], there).start()
    all_ref[m] = slots[...]
    for i, peer in enumerate(to_x):
        source = lax.rem(x + 3 - i, 4) * 2 + core
        copy(3, i, slots, all_ref.at[source], peer).wait_recv()
        copy(4, i + 1, all_ref.at[source], all_ref.at[source], there).start()
    copy(4, 0, slots, all_ref.at[sibling], there).wait_recv()
    for i, peer in enumerate(to_x):
        source = lax.rem(x + 3 - i, 4) * 2
        copy(4, i + 1, all_ref.at[source + core], all_ref.at[source + 1 - core], there).wait_recv()
    for i, peer in enumerate(to_x):
        source = lax.rem(x + 3 - i, 4) * 2
        copy(3, i, slots, all_ref.at[m], peer).wait_send()
        copy(4, i + 1, all_ref.at[source + core], all_ref.at[source + core], there).wait_send()
    copy(4, 0, slots, all_ref.at[m], there).wait_send()


def lanes(x, j):
    return jnp.broadcast_to(x[:, j : j + 1], x.shape)


def pivot_rows(rows_in, columns, k, lane, board):
    for j in range(8):
        board[8 * j : 8 * j + 8, :] = columns[j]
    board[64:72, :] = rows_in
    a = {}
    for j in range(8):
        for i in range(j, 8):
            a[i, j] = jnp.broadcast_to(board[8 * j + i : 8 * j + i + 1, :], (8, HALF))
    rows = [jnp.broadcast_to(board[64 + i : 65 + i, :], (8, HALF)) for i in range(8)]
    for j in range(0, 8, 2):
        p, q, d = a[j, j], a[j + 1, j], a[j + 1, j + 1]
        r = 1.0 / (p * d - q * q)
        pi, qi, di = d * r, -(q * r), p * r
        m0 = lane == k + j
        m1 = lane == k + j + 1
        both = m0 | m1
        r0 = jnp.where(both, jnp.where(m0, 1.0, 0.0), rows[j])
        r1 = jnp.where(both, jnp.where(m1, 1.0, 0.0), rows[j + 1])
        w0 = pi * r0 + qi * r1
        w1 = qi * r0 + di * r1
        rows[j], rows[j + 1] = w0, w1
        for i in range(8):
            if i in (j, j + 1):
                continue
            if i > j:
                rows[i] = jnp.where(both, 0.0, rows[i]) - (a[i, j] * w0 + a[i, j + 1] * w1)
            else:
                rows[i] = jnp.where(both, 0.0, rows[i]) + (a[j, i] * w0 + a[j + 1, i] * w1)
        old = dict(a)
        for n in range(j + 2, 8):
            u0 = pi * old[n, j] + qi * old[n, j + 1]
            u1 = qi * old[n, j] + di * old[n, j + 1]
            for i in range(n, 8):
                a[i, n] = old[i, n] - (old[i, j] * u0 + old[i, j + 1] * u1)
            for i in range(0, j):
                a[n, i] = old[n, i] - (old[j, i] * u0 + old[j + 1, i] * u1)
            a[n, j], a[n, j + 1] = -u0, -u1
    return rows


def invert(a_ref, board):
    lane = lax.broadcasted_iota(jnp.int32, (8, HALF), 1)
    sub = lax.broadcasted_iota(jnp.int32, (8, HALF), 0)
    n = HALF // 8
    a = [a_ref[8 * v : 8 * v + 8, :] for v in range(n)]
    lower, scaled = [], []
    for block in range(n):
        k = 8 * block
        columns = {v: [lanes(a[v], k + j) for j in range(8)] for v in range(block, n)}
        rows = pivot_rows(a[block], columns[block], k, lane, board.at[pl.ds(72 * block, 72)])
        here = (lane >= k) & (lane < k + 8)
        w = rows[0]
        for i in range(1, 8):
            w = jnp.where(sub == i, rows[i], w)
        scaled.append(jnp.where(lane < k + 8, w, 0.0))
        lower.append(jnp.where(lane < k, a[block], jnp.where(lane == k + sub, 1.0, 0.0)))
        for v in range(block + 1, n):
            t = [columns[v][j] * rows[j] for j in range(8)]
            s = ((t[0] + t[1]) + (t[2] + t[3])) + ((t[4] + t[5]) + (t[6] + t[7]))
            a[v] = jnp.where(here, 0.0, a[v]) - s
    return lax.dot_general(
        jnp.concatenate(lower, 0),
        jnp.concatenate(scaled, 0),
        (((0,), (0,)), ((), ())),
        precision=HIGHEST,
        preferred_element_type=jnp.float32,
    )


def row_of(all_ref, b, row):
    return all_ref[row // SLICE, b, row % SLICE : row % SLICE + 1, :]


def rows_of(all_ref, b, first, last):
    parts = []
    while first < last:
        s, r = first // SLICE, first % SLICE
        e = min(last - first, SLICE - r)
        parts.append(all_ref[s, b, r : r + e, :])
        first += e
    return jnp.concatenate(parts, 0)


def chain(all_ref, own_ref, ownrow_ref, blockrow_ref, slab_ref, post_ref, out_ref, pool, carry, turned, cosine, sine, half, board):
    batches = pool.shape[0]

    @pl.loop(0, batches)
    def _(b):
        pool[b] = rows_of(all_ref, b, 0, MEMBERS)

    post_ref[...] = own_ref[...]
    carry[...] = jnp.where(
        lax.broadcasted_iota(jnp.int32, carry.shape, 0) == lax.broadcasted_iota(jnp.int32, carry.shape, 1), 1.0, 0.0
    )

    @pl.loop(0, batches)
    def _(b):
        priors = pool[b]
        spread = priors - jnp.sum(priors, axis=0, keepdims=True) * (1.0 / MEMBERS)
        turned[...] = spread.T * (1.0 / (MEMBERS - 1))
        gap = rows_of(all_ref, b, MEMBERS, 2 * MEMBERS) - priors
        var = row_of(all_ref, b, VAR_ROW)
        cos = row_of(all_ref, b, COS_ROW)
        sin = row_of(all_ref, b, SIN_ROW)
        cosine[...] = jnp.broadcast_to(cos, (HALF, BATCH)).T
        sine[...] = jnp.broadcast_to(sin, (HALF, BATCH)).T
        st = turned[...]
        row = lax.broadcasted_iota(jnp.int32, (BATCH, HALF), 0)
        lane = lax.broadcasted_iota(jnp.int32, (BATCH, HALF), 1)

        def weight(c, s):
            return eighth(cosine[...] * c + sine[...] * s)

        def system(t):
            part = slice(t * HALF, t * HALF + HALF)
            w = weight(cos[:, part], sin[:, part])
            return w * dot(st, spread[:, part]) + jnp.where(row == lane + t * HALF, var[:, part], 0.0)

        left, right = system(0), system(1)
        a12 = right[:HALF]
        half[0] = left[:HALF]
        first = invert(half.at[0], board.at[0])
        both = dot(jnp.concatenate([left[HALF:], gap[:, :HALF]], 0), first)
        rest = jnp.concatenate([right[HALF:], gap[:, HALF:]], 0) - dot(both, a12)
        half[1] = rest[:HALF]
        second = invert(half.at[1], board.at[1])
        x2 = dot(rest[HALF:], second)
        x1 = both[HALF:] - dot(x2, both[:HALF])
        solved = jnp.concatenate([x1, x2], 1)

        def regress(field, c, s):
            g = weight(c, s) * dot(st, field)
            return field + dot(solved, g)

        @pl.loop(b + 1, batches)
        def _(k):
            c = row_of(all_ref, k, COS_ROW)
            s = row_of(all_ref, k, SIN_ROW)
            for t in range(2):
                part = slice(t * HALF, t * HALF + HALF)
                pool[k, :, part] = regress(pool[k, :, part], c[:, part], s[:, part])

        for t in range(2):
            part = slice(t * HALF, t * HALF + HALF)
            post_ref[:, part] = regress(post_ref[:, part], ownrow_ref[0:1, part], ownrow_ref[1:2, part])
        carry[...] = regress(carry[...], blockrow_ref[0:1, :], blockrow_ref[1:2, :])

    final = carry[...][:, :MEMBERS]
    for t in range(0, slab_ref.shape[1], BATCH):
        part = slice(t, t + BATCH)
        out_ref[:, part] = dot(final, slab_ref[:, part].astype(jnp.float32)).astype(jnp.bfloat16)


def call_chain(every, own, ownrow, blockrow, slab):
    vmem = pl.BlockSpec(memory_space=pltpu.VMEM)
    batches = every.shape[1]
    return pl.pallas_call(
        chain,
        out_shape=(
            jax.ShapeDtypeStruct(own.shape, jnp.float32),
            jax.ShapeDtypeStruct(slab.shape, jnp.bfloat16),
        ),
        in_specs=[vmem] * 5,
        out_specs=(vmem, vmem),
        scratch_shapes=[
            pltpu.VMEM((batches, MEMBERS, BATCH), jnp.float32),
            pltpu.VMEM((MEMBERS, HALF), jnp.float32),
            pltpu.VMEM((BATCH, MEMBERS), jnp.float32),
            pltpu.VMEM((BATCH, HALF), jnp.float32),
            pltpu.VMEM((BATCH, HALF), jnp.float32),
            pltpu.VMEM((2, HALF, HALF), jnp.float32),
            pltpu.VMEM((2, 72 * HALF // 8, HALF), jnp.float32),
        ],
        compiler_params=pltpu.CompilerParams(vmem_limit_bytes=48 << 20),
        name="chain",
    )(every, own, ownrow, blockrow, slab)


def shards(ensemble, obs_prior, obs_value, obs_var, obs_noise, obs_block, batch_owner):
    columns_n = lax.axis_size("col")
    column = lax.axis_index("col")
    member = lax.axis_index("mem")
    blocks_own = ensemble.shape[1]
    blocks = blocks_own * columns_n
    batches = batch_owner.shape[0]
    slab = lax.all_to_all(ensemble, "mem", split_axis=1, concat_axis=0, tiled=True)[:, 0, :]
    perturbed = obs_value[None, :] + jnp.sqrt(obs_var)[None, :] * obs_noise
    angle = obs_block.astype(jnp.float32) * (math.pi / blocks)
    cos, sin = jnp.cos(angle), jnp.sin(angle)
    packed = jnp.concatenate(
        [obs_prior, perturbed, obs_var[None], cos[None], sin[None], jnp.zeros((29, BATCH), jnp.float32)], 0
    )
    mine = lax.dynamic_slice_in_dim(packed, member * SLICE, SLICE, 0)
    vmem = pl.BlockSpec(memory_space=pltpu.VMEM)
    every = pl.pallas_call(
        exchange,
        out_shape=jax.ShapeDtypeStruct((8, batches, SLICE, BATCH), jnp.float32),
        in_specs=[vmem, pl.BlockSpec(memory_space=pltpu.SMEM)],
        out_specs=vmem,
        scratch_shapes=[
            pltpu.VMEM((8, SLICE, BATCH), jnp.float32),
            pltpu.VMEM((SLICE, BATCH), jnp.float32),
            pltpu.VMEM((8, SLICE, BATCH), jnp.float32),
            pltpu.VMEM((SLICE, BATCH), jnp.float32),
            pltpu.VMEM((batches, SLICE, BATCH), jnp.float32),
            pltpu.SemaphoreType.DMA((5, 7)),
            pltpu.SemaphoreType.DMA((5, 7)),
        ],
        compiler_params=pltpu.CompilerParams(collective_id=0, has_side_effects=True, vmem_limit_bytes=32 << 20),
        name="exchange",
    )(mine, batch_owner)
    block_angle = (column * blocks_own + member).astype(jnp.float32) * (math.pi / blocks)
    blockrow = jnp.broadcast_to(jnp.stack([jnp.cos(block_angle), jnp.sin(block_angle)])[:, None], (2, HALF))
    post, done = call_chain(every, obs_prior, jnp.stack([cos, sin]), blockrow, slab)
    analysis = lax.all_to_all(done[:, None, :], "mem", split_axis=0, concat_axis=1, tiled=True)
    return (analysis, post)


def solution(mesh):
    return jax.shard_map(
        shards,
        mesh=mesh,
        in_specs=(
            P("mem", "col", None),
            P(None, "col"),
            P("col"),
            P("col"),
            P(None, "col"),
            P("col"),
            P(),
        ),
        out_specs=(P("mem", "col", None), P(None, "col")),
        check_vma=False,
    )
```

```python
import functools
import math

import jax
import jax.numpy as jnp
from jax import lax
from jax.experimental import pallas as pl
from jax.experimental.pallas import tpu as pltpu
from jax.sharding import PartitionSpec as P

MESH = pl.DeviceIdType.MESH
HIGHEST = lax.Precision.HIGHEST
MEMBERS = 80
BATCH = 256
HALF = 128
GROUPS = 6
TILES = 8 * GROUPS


def dot(a, b, precision=HIGHEST):
    return jnp.dot(a, b, precision=precision, preferred_element_type=jnp.float32)


def eighth(x):
    x = x * x
    x = x * x
    return x * x


def lanes(x, j):
    return jnp.broadcast_to(x[:, j : j + 1], x.shape)


def pivot_rows(rows_in, columns, k, lane, board):
    for j in range(8):
        board[8 * j : 8 * j + 8, :] = columns[j]
    board[64:72, :] = rows_in
    a = {}
    for j in range(8):
        for i in range(j, 8):
            a[i, j] = jnp.broadcast_to(board[8 * j + i : 8 * j + i + 1, :], (8, HALF))
    rows = [jnp.broadcast_to(board[64 + i : 65 + i, :], (8, HALF)) for i in range(8)]
    for j in range(0, 8, 2):
        p, q, d = a[j, j], a[j + 1, j], a[j + 1, j + 1]
        r = 1.0 / (p * d - q * q)
        pi, qi, di = d * r, -(q * r), p * r
        m0 = lane == k + j
        m1 = lane == k + j + 1
        both = m0 | m1
        r0 = jnp.where(both, jnp.where(m0, 1.0, 0.0), rows[j])
        r1 = jnp.where(both, jnp.where(m1, 1.0, 0.0), rows[j + 1])
        w0 = pi * r0 + qi * r1
        w1 = qi * r0 + di * r1
        rows[j], rows[j + 1] = w0, w1
        for i in range(8):
            if i in (j, j + 1):
                continue
            if i > j:
                rows[i] = jnp.where(both, 0.0, rows[i]) - (a[i, j] * w0 + a[i, j + 1] * w1)
            else:
                rows[i] = jnp.where(both, 0.0, rows[i]) + (a[j, i] * w0 + a[j + 1, i] * w1)
        old = dict(a)
        for n in range(j + 2, 8):
            u0 = pi * old[n, j] + qi * old[n, j + 1]
            u1 = qi * old[n, j] + di * old[n, j + 1]
            for i in range(n, 8):
                a[i, n] = old[i, n] - (old[i, j] * u0 + old[i, j + 1] * u1)
            for i in range(0, j):
                a[n, i] = old[n, i] - (old[j, i] * u0 + old[j + 1, i] * u1)
            a[n, j], a[n, j + 1] = -u0, -u1
    return rows


def invert(a_ref, board):
    lane = lax.broadcasted_iota(jnp.int32, (8, HALF), 1)
    sub = lax.broadcasted_iota(jnp.int32, (8, HALF), 0)
    n = HALF // 8
    a = [a_ref[8 * v : 8 * v + 8, :] for v in range(n)]
    lower, scaled = [], []
    for block in range(n):
        k = 8 * block
        columns = {v: [lanes(a[v], k + j) for j in range(8)] for v in range(block, n)}
        rows = pivot_rows(a[block], columns[block], k, lane, board.at[pl.ds(72 * block, 72)])
        here = (lane >= k) & (lane < k + 8)
        w = rows[0]
        for i in range(1, 8):
            w = jnp.where(sub == i, rows[i], w)
        scaled.append(jnp.where(lane < k + 8, w, 0.0))
        lower.append(jnp.where(lane < k, a[block], jnp.where(lane == k + sub, 1.0, 0.0)))
        for v in range(block + 1, n):
            t = [columns[v][j] * rows[j] for j in range(8)]
            s = ((t[0] + t[1]) + (t[2] + t[3])) + ((t[4] + t[5]) + (t[6] + t[7]))
            a[v] = jnp.where(here, 0.0, a[v]) - s
    return lax.dot_general(
        jnp.concatenate(lower, 0),
        jnp.concatenate(scaled, 0),
        (((0,), (0,)), ((), ())),
        precision=HIGHEST,
        preferred_element_type=jnp.float32,
    )


def regress_all(
    ens_ref, prior_ref, value_ref, var_ref, noise_ref, angle_ref, block_ref, owner_ref,
    out_ref, post_ref,
    tiles, along_y, picked, along_z, along_z_rest, chosen, every, every_rest, wide, going, coming, back,
    state, pool, target, facts, carry, turned, cosine, sine, half, board, sends, recvs,
):
    m = lax.axis_index("mem")
    c = lax.axis_index("col")
    x, core = m // 2, lax.rem(m, 2)
    z, y = c // 8, lax.rem(c, 8)
    batches = pool.shape[0]
    rows = ens_ref.shape[0]
    to_y = [(m, z * 8 + lax.rem(y + i, 8)) for i in range(1, 8)]
    to_z = [(m, lax.rem(z + i, 8) * 8 + y) for i in range(1, 8)]
    to_m = [(lax.rem(m + i, 8), c) for i in range(1, 8)]
    to_x = [(lax.rem(x + i, 4) * 2 + core, c) for i in range(1, 4)]
    there = (x * 2 + 1 - core, c)
    barrier = pltpu.get_barrier_semaphore()
    for peer in to_y + to_z + to_m:
        pl.semaphore_signal(barrier, inc=1, device_id=peer, device_id_type=MESH)

    cos, sin = jnp.cos(angle_ref[...]), jnp.sin(angle_ref[...])
    perturbed = value_ref[...] + jnp.sqrt(var_ref[...]) * noise_ref[...]
    for g in range(10):
        for t in range(2):
            lane = slice(t * HALF, t * HALF + HALF)
            tiles[2 * g + t] = prior_ref[8 * g : 8 * g + 8, lane]
            tiles[20 + 2 * g + t] = perturbed[8 * g : 8 * g + 8, lane]
    for t in range(2):
        lane = slice(t * HALF, t * HALF + HALF)
        tiles[40 + t] = jnp.concatenate(
            [var_ref[:, lane], cos[:, lane], sin[:, lane], jnp.zeros((5, HALF), jnp.float32)], 0
        )
    for t in range(42, TILES):
        tiles[t] = jnp.zeros((8, HALF), jnp.float32)
    pl.semaphore_wait(barrier, 21)

    def copy(phase, i, src, dst, peer):
        return pltpu.make_async_remote_copy(
            src_ref=src,
            dst_ref=dst,
            send_sem=sends.at[phase, i],
            recv_sem=recvs.at[phase, i],
            device_id=peer,
            device_id_type=MESH,
        )

    piece = lambda k: tiles.at[m * GROUPS + jnp.minimum(k, GROUPS - 1)]
    for i, peer in enumerate(to_y):
        copy(0, i, piece(lax.rem(y + i + 1, 8)), along_y.at[y], peer).start()
    along_y[y] = tiles[m * GROUPS + jnp.minimum(y, GROUPS - 1)]

    wide[...] = ens_ref[...].astype(jnp.float32)
    for g in range(8):
        going[g] = wide[:, g, :].astype(jnp.bfloat16)

    def wait_recv(phase, i, src, dst, peer):
        copy(phase, i, src, dst, peer).wait_recv()

    for i, peer in enumerate(to_y):
        wait_recv(0, i, tiles.at[0], along_y.at[lax.rem(y + 7 - i, 8)], peer)
    owners = [owner_ref[j] for j in range(batches)]
    for j in range(batches):
        picked[j] = along_y[lax.rem(owners[j], 8)]
    rest = pl.ds(1, batches - 1)
    for i, peer in enumerate(to_z):
        copy(1, i, picked.at[0], along_z.at[z], peer).start()
    for i, peer in enumerate(to_z):
        copy(2, i, picked.at[rest], along_z_rest.at[z], peer).start()
    along_z[z] = picked[0]
    along_z_rest[z] = picked[1:]
    for i, peer in enumerate(to_z):
        wait_recv(1, i, picked.at[0], along_z.at[lax.rem(z + 7 - i, 8)], peer)
    chosen[0] = along_z[owners[0] // 8]
    for i, peer in enumerate(to_y):
        copy(3, i, chosen.at[0], every.at[m, y], peer).start()
    every[m, y] = chosen[0]
    for i, peer in enumerate(to_y):
        wait_recv(3, i, chosen.at[0], every.at[m, lax.rem(y + 7 - i, 8)], peer)
    used = pl.ds(0, GROUPS)
    mine = every.at[m, used]
    for i, peer in enumerate(to_x):
        copy(4, i, mine, mine, peer).start()
    copy(5, 0, mine, mine, there).start()

    for i, peer in enumerate(to_z):
        wait_recv(2, i, picked.at[rest], along_z_rest.at[lax.rem(z + 7 - i, 8)], peer)
    for j in range(1, batches):
        chosen[j] = along_z_rest[owners[j] // 8, j - 1]
    for i, peer in enumerate(to_y):
        copy(6, i, chosen.at[rest], every_rest.at[m, y], peer).start()
    every_rest[m, y] = chosen[1:]

    def source(i):
        return lax.rem(x + 3 - i, 4) * 2

    for i, peer in enumerate(to_x):
        got = every.at[source(i) + core, used]
        wait_recv(4, i, got, got, peer)
        copy(5, i + 1, got, got, there).start()
    for i, peer in enumerate(to_m):
        copy(9, i, going.at[lax.rem(m + i + 1, 8)], coming.at[m], peer).start()
    coming[m] = going[m]
    wait_recv(5, 0, mine, every.at[there[0], used], there)
    for i, peer in enumerate(to_x):
        got = every.at[source(i) + 1 - core, used]
        wait_recv(5, i + 1, got, got, there)

    def unpack(get, b):
        for t in range(40):
            g, lane = t % 20 // 2, slice(t % 2 * HALF, t % 2 * HALF + HALF)
            to = pool if t < 20 else target
            to[b, 8 * g : 8 * g + 8, lane] = get(t // GROUPS, t % GROUPS)
        for t in range(40, 42):
            lane = slice(t % 2 * HALF, t % 2 * HALF + HALF)
            facts[b, :, lane] = get(t // GROUPS, t % GROUPS)

    unpack(lambda p, q: every[p, q], 0)
    post_ref[...] = prior_ref[...]
    carry[...] = jnp.where(
        lax.broadcasted_iota(jnp.int32, carry.shape, 0) == lax.broadcasted_iota(jnp.int32, carry.shape, 1), 1.0, 0.0
    )

    @pl.loop(0, batches)
    def _(b):
        priors = pool[b]
        spread = priors - jnp.sum(priors, axis=0, keepdims=True) * (1.0 / MEMBERS)
        turned[...] = spread.T * (1.0 / (MEMBERS - 1))
        gap = target[b] - priors
        fact = facts[b]
        var, cos, sin = fact[0:1], fact[1:2], fact[2:3]
        cosine[...] = jnp.broadcast_to(cos, (HALF, BATCH)).T
        sine[...] = jnp.broadcast_to(sin, (HALF, BATCH)).T
        st = turned[...]
        row = lax.broadcasted_iota(jnp.int32, (BATCH, HALF), 0)
        lane = lax.broadcasted_iota(jnp.int32, (BATCH, HALF), 1)

        def weight(c, s):
            return eighth(cosine[...] * c + sine[...] * s)

        def system(t):
            part = slice(t * HALF, t * HALF + HALF)
            w = weight(cos[:, part], sin[:, part])
            return w * dot(st, spread[:, part]) + jnp.where(row == lane + t * HALF, var[:, part], 0.0)

        left, right = system(0), system(1)
        a12 = right[:HALF]
        half[0] = left[:HALF]

        @pl.when(b == 0)
        def _():
            for i, peer in enumerate(to_y):
                wait_recv(6, i, chosen.at[rest], every_rest.at[m, lax.rem(y + 7 - i, 8)], peer)
            part = every_rest.at[m, used]
            for i, peer in enumerate(to_x):
                copy(7, i, part, part, peer).start()
            copy(8, 0, part, part, there).start()

        first = invert(half.at[0], board.at[0])
        both = dot(jnp.concatenate([left[HALF:], gap[:, :HALF]], 0), first)
        schur = jnp.concatenate([right[HALF:], gap[:, HALF:]], 0) - dot(both, a12)
        half[1] = schur[:HALF]
        second = invert(half.at[1], board.at[1])

        @pl.when(b == 0)
        def _():
            for i, peer in enumerate(to_x):
                got = every_rest.at[source(i) + core, used]
                wait_recv(7, i, got, got, peer)
                copy(8, i + 1, got, got, there).start()

        x2 = dot(schur[HALF:], second)
        x1 = both[HALF:] - dot(x2, both[:HALF])
        solved = jnp.concatenate([x1, x2], 1)

        def regress(field, c, s):
            g = weight(c, s) * dot(st, field)
            return field + dot(solved, g)

        for t in range(2):
            part = slice(t * HALF, t * HALF + HALF)
            c, s = tiles[40 + t][1:2], tiles[40 + t][2:3]
            post_ref[:, part] = regress(post_ref[:, part], c, s)
        carry[...] = regress(carry[...], block_ref[0:1, :], block_ref[1:2, :])

        @pl.when(b == 0)
        def _():
            wait_recv(8, 0, every_rest.at[m, used], every_rest.at[there[0], used], there)
            for i, peer in enumerate(to_x):
                got = every_rest.at[source(i) + 1 - core, used]
                wait_recv(8, i + 1, got, got, there)

            @pl.loop(1, batches)
            def _(k):
                unpack(lambda p, q: every_rest[p, q, k - 1], k)

            for i, peer in enumerate(to_m):
                wait_recv(9, i, going.at[0], coming.at[lax.rem(m + 7 - i, 8)], peer)
            for g in range(8):
                state[rows * g : rows * g + rows, :] = coming[g].astype(jnp.float32)

        @pl.loop(b + 1, batches)
        def _(k):
            c = facts[k][1:2]
            s = facts[k][2:3]
            for t in range(2):
                part = slice(t * HALF, t * HALF + HALF)
                pool[k, :, part] = regress(pool[k, :, part], c[:, part], s[:, part])

    for i, peer in enumerate(to_y):
        copy(0, i, tiles.at[0], along_y.at[y], peer).wait_send()
        copy(3, i, chosen.at[0], every.at[m, y], peer).wait_send()
        copy(6, i, chosen.at[rest], every_rest.at[m, y], peer).wait_send()
    for i, peer in enumerate(to_z):
        copy(1, i, picked.at[0], along_z.at[z], peer).wait_send()
        copy(2, i, picked.at[rest], along_z_rest.at[z], peer).wait_send()
    part = every_rest.at[m, used]
    for i, peer in enumerate(to_x):
        copy(4, i, mine, mine, peer).wait_send()
        copy(7, i, part, part, peer).wait_send()
    for i in range(4):
        copy(5, i, mine, mine, there).wait_send()
        copy(8, i, part, part, there).wait_send()
    for i, peer in enumerate(to_m):
        copy(9, i, going.at[0], coming.at[m], peer).wait_send()

    final = carry[...][:, :MEMBERS]
    for t in range(0, state.shape[1], BATCH):
        part = slice(t, t + BATCH)
        state[:, part] = dot(final, state[:, part])
    for g in range(8):
        going[g] = state[rows * g : rows * g + rows, :].astype(jnp.bfloat16)
    for i, peer in enumerate(to_m):
        copy(10, i, going.at[lax.rem(m + i + 1, 8)], back.at[m], peer).start()
    back[m] = going[m]
    for i, peer in enumerate(to_m):
        one = copy(10, i, going.at[0], back.at[lax.rem(m + 7 - i, 8)], peer)
        one.wait_recv()
        one.wait_send()
    for g in range(8):
        wide[:, g, :] = back[g].astype(jnp.float32)
    out_ref[...] = wide[...].astype(jnp.bfloat16)


def shards(ensemble, obs_prior, obs_value, obs_var, obs_noise, obs_block, batch_owner):
    columns_n = lax.axis_size("col")
    column = lax.axis_index("col")
    member = lax.axis_index("mem")
    rows, blocks_own, cells = ensemble.shape
    blocks = blocks_own * columns_n
    batches = batch_owner.shape[0]
    angle = obs_block.astype(jnp.float32) * (math.pi / blocks)
    block_angle = (column * blocks_own + member).astype(jnp.float32) * (math.pi / blocks)
    blockrow = jnp.broadcast_to(jnp.stack([jnp.cos(block_angle), jnp.sin(block_angle)])[:, None], (2, HALF))
    vmem = pl.BlockSpec(memory_space=pltpu.VMEM)
    f32, bf16 = jnp.float32, jnp.bfloat16
    return pl.pallas_call(
        regress_all,
        out_shape=(
            jax.ShapeDtypeStruct(ensemble.shape, bf16),
            jax.ShapeDtypeStruct(obs_prior.shape, f32),
        ),
        in_specs=[vmem] * 7 + [pl.BlockSpec(memory_space=pltpu.SMEM)],
        out_specs=(vmem, vmem),
        scratch_shapes=[
            pltpu.VMEM((TILES, 8, HALF), f32),
            pltpu.VMEM((8, 8, HALF), f32),
            pltpu.VMEM((batches, 8, HALF), f32),
            pltpu.VMEM((8, 8, HALF), f32),
            pltpu.VMEM((8, batches - 1, 8, HALF), f32),
            pltpu.VMEM((batches, 8, HALF), f32),
            pltpu.VMEM((8, 8, 8, HALF), f32),
            pltpu.VMEM((8, 8, batches - 1, 8, HALF), f32),
            pltpu.VMEM(ensemble.shape, f32),
            pltpu.VMEM((8, rows, cells), bf16),
            pltpu.VMEM((8, rows, cells), bf16),
            pltpu.VMEM((8, rows, cells), bf16),
            pltpu.VMEM((MEMBERS, cells), f32),
            pltpu.VMEM((batches, MEMBERS, BATCH), f32),
            pltpu.VMEM((batches, MEMBERS, BATCH), f32),
            pltpu.VMEM((batches, 8, BATCH), f32),
            pltpu.VMEM((MEMBERS, HALF), f32),
            pltpu.VMEM((BATCH, MEMBERS), f32),
            pltpu.VMEM((BATCH, HALF), f32),
            pltpu.VMEM((BATCH, HALF), f32),
            pltpu.VMEM((2, HALF, HALF), f32),
            pltpu.VMEM((2, 72 * HALF // 8, HALF), f32),
            pltpu.SemaphoreType.DMA((11, 7)),
            pltpu.SemaphoreType.DMA((11, 7)),
        ],
        compiler_params=pltpu.CompilerParams(collective_id=0, has_side_effects=True, vmem_limit_bytes=48 << 20),
        name="regress_all",
    )(
        ensemble, obs_prior, obs_value[None], obs_var[None], obs_noise, angle[None], blockrow, batch_owner
    )


def solution(mesh):
    return jax.shard_map(
        shards,
        mesh=mesh,
        in_specs=(
            P("mem", "col", None),
            P(None, "col"),
            P("col"),
            P("col"),
            P(None, "col"),
            P("col"),
            P(),
        ),
        out_specs=(P("mem", "col", None), P(None, "col")),
        check_vma=False,
    )
```

```python
import functools
import math

import jax
import jax.numpy as jnp
from jax import lax
from jax.experimental import pallas as pl
from jax.experimental.pallas import tpu as pltpu
from jax.sharding import PartitionSpec as P

MESH = pl.DeviceIdType.MESH
MEMBERS = 80
BATCH = 256
HALF = 128
GROUPS = 6
TILES = 8 * GROUPS


def split(x, n):
    parts = []
    for _ in range(n - 1):
        parts.append(x.astype(jnp.bfloat16))
        x = x - parts[-1].astype(jnp.float32)
    parts.append(x.astype(jnp.bfloat16))
    return parts


def once(a, b):
    return jnp.dot(a, b, preferred_element_type=jnp.float32)


def cat0(*v):
    return jnp.concatenate(v, 0)


def cat1(*v):
    return jnp.concatenate(v, 1)


def narrow(a, b):
    p, q = split(a, 3), split(b, 3)
    front = cat1(p[0], p[1])
    return (once(cat1(p[0], p[2]), cat0(q[2], q[0])) + once(front, cat0(q[1], q[1]))) + once(front, cat0(q[0], q[0]))


def wide_sum(stack, n, q):
    top = once(stack, q[0])
    middle = once(stack[: 2 * n], q[1])
    low = once(stack[:n], q[2])
    return top[:n] + ((top[n : 2 * n] + middle[:n]) + (top[2 * n :] + middle[n:] + low))


def eighth(x):
    x = x * x
    x = x * x
    return x * x


def lanes(x, j):
    return jnp.broadcast_to(x[:, j : j + 1], x.shape)


def pivot_rows(rows_in, columns, k, lane, board):
    for j in range(8):
        board[8 * j : 8 * j + 8, :] = columns[j]
    board[64:72, :] = rows_in
    a = {}
    for j in range(8):
        for i in range(j, 8):
            a[i, j] = jnp.broadcast_to(board[8 * j + i : 8 * j + i + 1, :], (8, HALF))
    rows = [jnp.broadcast_to(board[64 + i : 65 + i, :], (8, HALF)) for i in range(8)]
    for j in range(0, 8, 2):
        p, q, d = a[j, j], a[j + 1, j], a[j + 1, j + 1]
        r = 1.0 / (p * d - q * q)
        pi, qi, di = d * r, -(q * r), p * r
        m0 = lane == k + j
        m1 = lane == k + j + 1
        both = m0 | m1
        r0 = jnp.where(both, jnp.where(m0, 1.0, 0.0), rows[j])
        r1 = jnp.where(both, jnp.where(m1, 1.0, 0.0), rows[j + 1])
        w0 = pi * r0 + qi * r1
        w1 = qi * r0 + di * r1
        rows[j], rows[j + 1] = w0, w1
        for i in range(8):
            if i in (j, j + 1):
                continue
            if i > j:
                rows[i] = jnp.where(both, 0.0, rows[i]) - (a[i, j] * w0 + a[i, j + 1] * w1)
            else:
                rows[i] = jnp.where(both, 0.0, rows[i]) + (a[j, i] * w0 + a[j + 1, i] * w1)
        old = dict(a)
        for n in range(j + 2, 8):
            u0 = pi * old[n, j] + qi * old[n, j + 1]
            u1 = qi * old[n, j] + di * old[n, j + 1]
            for i in range(n, 8):
                a[i, n] = old[i, n] - (old[i, j] * u0 + old[i, j + 1] * u1)
            for i in range(0, j):
                a[n, i] = old[n, i] - (old[j, i] * u0 + old[j + 1, i] * u1)
            a[n, j], a[n, j + 1] = -u0, -u1
    return rows

def invert(a_ref, board, between):
    lane = lax.broadcasted_iota(jnp.int32, (8, HALF), 1)
    sub = lax.broadcasted_iota(jnp.int32, (8, HALF), 0)
    n = HALF // 8
    a = [a_ref[8 * v : 8 * v + 8, :] for v in range(n)]
    lower, scaled = [], []
    for block in range(n):
        k = 8 * block
        columns = {v: [lanes(a[v], k + j) for j in range(8)] for v in range(block, n)}
        rows = pivot_rows(a[block], columns[block], k, lane, board.at[pl.ds(72 * block, 72)])
        here = (lane >= k) & (lane < k + 8)
        w = rows[0]
        for i in range(1, 8):
            w = jnp.where(sub == i, rows[i], w)
        scaled.append(jnp.where(lane < k + 8, w, 0.0))
        lower.append(jnp.where(lane < k, a[block], jnp.where(lane == k + sub, 1.0, 0.0)))
        for v in range(block + 1, n):
            t = [columns[v][j] * rows[j] for j in range(8)]
            s = ((t[0] + t[1]) + (t[2] + t[3])) + ((t[4] + t[5]) + (t[6] + t[7]))
            a[v] = jnp.where(here, 0.0, a[v]) - s
        between()
    return narrow(jnp.concatenate(lower, 0).T, jnp.concatenate(scaled, 0))


class Regression:
    def __init__(self, p, turned, turned_low, cosine, sine, solved, gains):
        self.p = p
        self.turned, self.turned_low, self.cosine, self.sine = turned, turned_low, cosine, sine
        self.solved, self.gains = solved, gains

    def weight(self, c, s):
        return eighth(self.cosine[self.p] * c + self.sine[self.p] * s)

    def across(self, field):
        f = split(field, 3)
        total = once(self.turned_low[self.p], cat0(f[1], f[0], f[2])) + once(self.turned[self.p], cat0(f[0], f[0], f[1]))
        return total * (1.0 / (MEMBERS - 1))

    def gain(self, i, field, c, s):
        for q, part in enumerate(split(self.weight(c, s) * self.across(field), 3)):
            self.gains[i, q] = part

    def add(self, i, field):
        return field + wide_sum(self.solved[self.p], MEMBERS, [self.gains[i, q] for q in range(3)])


def later(regression, fields):
    for i, (read, write, c, s) in enumerate(fields):
        regression.gain(i % 2, read(), c(), s())
        yield
        write(regression.add(i % 2, read()))
        yield


def columns_of(ref, k, facts):
    for t in range(2):
        part = slice(t * HALF, t * HALF + HALF)

        def write(value, part=part):
            ref[k, :, part] = value

        yield (
            lambda part=part: ref[k, :, part],
            write,
            lambda part=part: facts[k, 1:2, part],
            lambda part=part: facts[k, 2:3, part],
        )


def assimilate(batches, pool, target, facts, carry, blockrow, turned, turned_low, cosine, sine, solved, gains, half, board, hooks):
    own = pool.shape[0] - 1
    turned[1] = jnp.zeros(turned.shape[1:], turned.dtype)
    turned_low[1] = jnp.zeros(turned.shape[1:], turned.dtype)
    cosine[1] = jnp.zeros(cosine.shape[1:], jnp.float32)
    sine[1] = jnp.zeros(cosine.shape[1:], jnp.float32)
    solved[1] = jnp.zeros(solved.shape[1:], solved.dtype)
    row = lax.broadcasted_iota(jnp.int32, carry.shape, 0)
    carry[...] = jnp.where(row == lax.broadcasted_iota(jnp.int32, carry.shape, 1), 1.0, 0.0)

    def keep(value):
        carry[...] = value

    mine = list(columns_of(pool, own, facts)) + [
        (lambda: carry[...], keep, lambda: blockrow[0:1, :], lambda: blockrow[1:2, :])
    ]
    factors = (turned, turned_low, cosine, sine, solved, gains)

    @pl.loop(0, batches)
    def _(b):
        now = lax.rem(b, 2)
        here = Regression(now, *factors)
        before = Regression(1 - now, *factors)
        priors = pool[b]
        spread = priors - jnp.sum(priors, axis=0, keepdims=True) * (1.0 / MEMBERS)
        s0, s1, s2 = split(spread, 3)
        turned[now] = cat0(s0, s1, s0).T
        turned_low[now] = cat0(s1, s2, s0).T
        gap = target[b] - priors
        fact = facts[b]
        var, cos, sin = fact[0:1], fact[1:2], fact[2:3]
        cosine[now] = jnp.broadcast_to(cos, (HALF, BATCH)).T
        sine[now] = jnp.broadcast_to(sin, (HALF, BATCH)).T
        row = lax.broadcasted_iota(jnp.int32, (BATCH, HALF), 0)
        lane = lax.broadcasted_iota(jnp.int32, (BATCH, HALF), 1)
        covariance = here.across(spread)

        def system(t):
            part = slice(t * HALF, t * HALF + HALF)
            w = here.weight(cos[:, part], sin[:, part])
            return w * covariance[:, part] + jnp.where(row == lane + t * HALF, var[:, part], 0.0)

        left, right = system(0), system(1)
        a12 = right[:HALF]
        half[0] = left[:HALF]
        hooks[0](b)
        fields = list(mine)
        for i in range(batches - 2):
            fields += columns_of(pool, b + 2 - 1 + i, facts)
        steps = later(before, fields)
        done = object()
        between = lambda: next(steps, done)
        first = invert(half.at[0], board.at[0], between)
        both = narrow(cat0(left[HALF:], gap[:, :HALF]), first)
        schur = cat0(right[HALF:], gap[:, HALF:]) - narrow(both, a12)
        half[1] = schur[:HALF]
        second = invert(half.at[1], board.at[1], between)
        for _ in steps:
            pass
        hooks[1](b)
        x2 = narrow(schur[HALF:], second)
        x1 = both[HALF:] - narrow(x2, both[:HALF])
        solved[now] = cat0(*split(cat1(x1, x2), 3))
        hooks[2](b)
        for _ in later(here, columns_of(pool, b + 1, facts)):
            pass

    return Regression((batches - 1) % 2, *factors), mine


def regress_all(
    ens_hbm, prior_hbm, value_hbm, var_hbm, noise_hbm, place_hbm, owner_ref,
    out_ref, post_ref,
    ens, prior, value, var_in, noise, place, blockrow,
    tiles, along_y, picked, along_z, along_z_rest, chosen, every, every_rest, wide, going, coming, back,
    state, pool, target, facts, carry, turned, turned_low, cosine, sine, solved, gains, half, board,
    loads, sends, recvs,
):
    m = lax.axis_index("mem")
    c = lax.axis_index("col")
    x, core = m // 2, lax.rem(m, 2)
    z, y = c // 8, lax.rem(c, 8)
    batches = target.shape[0]
    own = pool.shape[0] - 1
    rows, blocks_own, _ = ens.shape
    step = math.pi / (blocks_own * lax.axis_size("col"))
    arrived = [
        pltpu.make_async_copy(far, near, loads.at[i])
        for i, (far, near) in enumerate(
            [
                (value_hbm, value),
                (var_hbm, var_in),
                (place_hbm, place),
                (prior_hbm, prior),
                (noise_hbm, noise),
                (ens_hbm, ens),
            ]
        )
    ]
    for load in arrived:
        load.start()
    to_y = [(m, z * 8 + lax.rem(y + i, 8)) for i in range(1, 8)]
    to_z = [(m, lax.rem(z + i, 8) * 8 + y) for i in range(1, 8)]
    to_m = [(lax.rem(m + i, 8), c) for i in range(1, 8)]
    to_x = [(lax.rem(x + i, 4) * 2 + core, c) for i in range(1, 4)]
    there = (x * 2 + 1 - core, c)
    barrier = pltpu.get_barrier_semaphore()
    for peer in to_y + to_z + to_m:
        pl.semaphore_signal(barrier, inc=1, device_id=peer, device_id_type=MESH)

    here = jnp.full((8, HALF), (c * blocks_own + m).astype(jnp.float32) * step)
    blockrow[...] = jnp.where(lax.broadcasted_iota(jnp.int32, (8, HALF), 0) == 0, jnp.cos(here), jnp.sin(here))
    for t in range(42, TILES):
        tiles[t] = jnp.zeros((8, HALF), jnp.float32)
    for load in arrived[:5]:
        load.wait()
    angle = place[...].astype(jnp.float32) * step
    cos, sin = jnp.cos(angle), jnp.sin(angle)
    perturbed = value[...] + jnp.sqrt(var_in[...]) * noise[...]
    for g in range(10):
        for t in range(2):
            lane = slice(t * HALF, t * HALF + HALF)
            tiles[2 * g + t] = prior[8 * g : 8 * g + 8, lane]
            tiles[20 + 2 * g + t] = perturbed[8 * g : 8 * g + 8, lane]
    fact = jnp.concatenate([var_in[...], cos, sin, jnp.zeros((5, BATCH), jnp.float32)], 0)
    for t in range(2):
        tiles[40 + t] = fact[:, t * HALF : t * HALF + HALF]
    pl.semaphore_wait(barrier, 21)

    def copy(phase, i, src, dst, peer):
        return pltpu.make_async_remote_copy(
            src_ref=src,
            dst_ref=dst,
            send_sem=sends.at[phase, i],
            recv_sem=recvs.at[phase, i],
            device_id=peer,
            device_id_type=MESH,
        )

    piece = lambda k: tiles.at[m * GROUPS + jnp.minimum(k, GROUPS - 1)]
    for i, peer in enumerate(to_y):
        copy(0, i, piece(lax.rem(y + i + 1, 8)), along_y.at[y], peer).start()
    along_y[y] = tiles[m * GROUPS + jnp.minimum(y, GROUPS - 1)]

    arrived[5].wait()
    wide[...] = ens[...].astype(jnp.float32)
    for g in range(8):
        going[g] = wide[:, g, :].astype(jnp.bfloat16)

    for b in range(batches, own):
        pool[b] = jnp.zeros(pool.shape[1:], jnp.float32)
        facts[b] = jnp.zeros(facts.shape[1:], jnp.float32)
    pool[own] = prior[...]
    facts[own] = fact

    def wait_recv(phase, i, src, dst, peer):
        copy(phase, i, src, dst, peer).wait_recv()

    for i, peer in enumerate(to_y):
        wait_recv(0, i, tiles.at[0], along_y.at[lax.rem(y + 7 - i, 8)], peer)
    owners = [owner_ref[j] for j in range(batches)]
    for j in range(batches):
        picked[j] = along_y[lax.rem(owners[j], 8)]
    rest = pl.ds(1, batches - 1)
    for i, peer in enumerate(to_z):
        copy(1, i, picked.at[0], along_z.at[z], peer).start()
    for i, peer in enumerate(to_z):
        copy(2, i, picked.at[rest], along_z_rest.at[z], peer).start()
    along_z[z] = picked[0]
    along_z_rest[z] = picked[1:]
    for i, peer in enumerate(to_z):
        wait_recv(1, i, picked.at[0], along_z.at[lax.rem(z + 7 - i, 8)], peer)
    chosen[0] = along_z[owners[0] // 8]
    for i, peer in enumerate(to_y):
        copy(3, i, chosen.at[0], every.at[m, y], peer).start()
    every[m, y] = chosen[0]
    for i, peer in enumerate(to_y):
        wait_recv(3, i, chosen.at[0], every.at[m, lax.rem(y + 7 - i, 8)], peer)
    used = pl.ds(0, GROUPS)
    mine = every.at[m, used]
    for i, peer in enumerate(to_x):
        copy(4, i, mine, mine, peer).start()
    copy(5, 0, mine, mine, there).start()

    for i, peer in enumerate(to_z):
        wait_recv(2, i, picked.at[rest], along_z_rest.at[lax.rem(z + 7 - i, 8)], peer)
    for j in range(1, batches):
        chosen[j] = along_z_rest[owners[j] // 8, j - 1]
    for i, peer in enumerate(to_y):
        copy(6, i, chosen.at[rest], every_rest.at[m, y], peer).start()
    every_rest[m, y] = chosen[1:]

    def source(i):
        return lax.rem(x + 3 - i, 4) * 2

    for i, peer in enumerate(to_x):
        got = every.at[source(i) + core, used]
        wait_recv(4, i, got, got, peer)
        copy(5, i + 1, got, got, there).start()
    for i, peer in enumerate(to_m):
        copy(9, i, going.at[lax.rem(m + i + 1, 8)], coming.at[m], peer).start()
    coming[m] = going[m]
    wait_recv(5, 0, mine, every.at[there[0], used], there)
    for i, peer in enumerate(to_x):
        got = every.at[source(i) + 1 - core, used]
        wait_recv(5, i + 1, got, got, there)

    def unpack(get, b):
        for t in range(40):
            g, lane = t % 20 // 2, slice(t % 2 * HALF, t % 2 * HALF + HALF)
            to = pool if t < 20 else target
            to[b, 8 * g : 8 * g + 8, lane] = get(t // GROUPS, t % GROUPS)
        for t in range(40, 42):
            lane = slice(t % 2 * HALF, t % 2 * HALF + HALF)
            facts[b, :, lane] = get(t // GROUPS, t % GROUPS)

    unpack(lambda p, q: every[p, q], 0)
    def spread_rest(b):
        @pl.when(b == 0)
        def _():
            for i, peer in enumerate(to_y):
                wait_recv(6, i, chosen.at[rest], every_rest.at[m, lax.rem(y + 7 - i, 8)], peer)
            part = every_rest.at[m, used]
            for i, peer in enumerate(to_x):
                copy(7, i, part, part, peer).start()
            copy(8, 0, part, part, there).start()

    def forward_rest(b):
        @pl.when(b == 0)
        def _():
            for i, peer in enumerate(to_x):
                got = every_rest.at[source(i) + core, used]
                wait_recv(7, i, got, got, peer)
                copy(8, i + 1, got, got, there).start()

    def take_rest(b):
        @pl.when(b == 0)
        def _():
            wait_recv(8, 0, every_rest.at[m, used], every_rest.at[there[0], used], there)
            for i, peer in enumerate(to_x):
                got = every_rest.at[source(i) + 1 - core, used]
                wait_recv(8, i + 1, got, got, there)

            @pl.loop(1, batches)
            def _(k):
                unpack(lambda p, q: every_rest[p, q, k - 1], k)

            for i, peer in enumerate(to_m):
                wait_recv(9, i, going.at[0], coming.at[lax.rem(m + 7 - i, 8)], peer)
            for g in range(8):
                state[rows * g : rows * g + rows, :] = coming[g].astype(jnp.float32)

    last, fields = assimilate(
        batches, pool, target, facts, carry, blockrow, turned, turned_low, cosine, sine, solved, gains, half, board,
        (spread_rest, forward_rest, take_rest),
    )

    for i, peer in enumerate(to_y):
        copy(0, i, tiles.at[0], along_y.at[y], peer).wait_send()
        copy(3, i, chosen.at[0], every.at[m, y], peer).wait_send()
        copy(6, i, chosen.at[rest], every_rest.at[m, y], peer).wait_send()
    for i, peer in enumerate(to_z):
        copy(1, i, picked.at[0], along_z.at[z], peer).wait_send()
        copy(2, i, picked.at[rest], along_z_rest.at[z], peer).wait_send()
    part = every_rest.at[m, used]
    for i, peer in enumerate(to_x):
        copy(4, i, mine, mine, peer).wait_send()
        copy(7, i, part, part, peer).wait_send()
    for i in range(4):
        copy(5, i, mine, mine, there).wait_send()
        copy(8, i, part, part, there).wait_send()
    for i, peer in enumerate(to_m):
        copy(9, i, going.at[0], coming.at[m], peer).wait_send()

    for _ in later(last, fields[2:]):
        pass
    final = cat1(*split(carry[...][:, :MEMBERS], 3))
    for t in range(0, state.shape[1], BATCH):
        part = slice(t, t + BATCH)
        f = state[:, part].astype(jnp.bfloat16)
        state[:, part] = once(final, cat0(f, f, f))
    for g in range(8):
        going[g] = state[rows * g : rows * g + rows, :].astype(jnp.bfloat16)
    for i, peer in enumerate(to_m):
        copy(10, i, going.at[lax.rem(m + i + 1, 8)], back.at[m], peer).start()
    back[m] = going[m]
    for _ in later(last, fields[:2]):
        pass
    post_ref[...] = pool[own]
    for i, peer in enumerate(to_m):
        one = copy(10, i, going.at[0], back.at[lax.rem(m + 7 - i, 8)], peer)
        one.wait_recv()
        one.wait_send()
    for g in range(8):
        wide[:, g, :] = back[g].astype(jnp.float32)
    out_ref[...] = wide[...].astype(jnp.bfloat16)


def shards(ensemble, obs_prior, obs_value, obs_var, obs_noise, obs_block, batch_owner):
    rows, _, cells = ensemble.shape
    batches = batch_owner.shape[0]
    vmem = pl.BlockSpec(memory_space=pltpu.VMEM)
    f32, bf16 = jnp.float32, jnp.bfloat16
    return pl.pallas_call(
        regress_all,
        out_shape=(
            jax.ShapeDtypeStruct(ensemble.shape, bf16),
            jax.ShapeDtypeStruct(obs_prior.shape, f32),
        ),
        in_specs=[pl.BlockSpec(memory_space=pltpu.HBM)] * 6 + [pl.BlockSpec(memory_space=pltpu.SMEM)],
        out_specs=(vmem, vmem),
        scratch_shapes=[
            pltpu.VMEM(ensemble.shape, bf16),
            pltpu.VMEM(obs_prior.shape, f32),
            pltpu.VMEM((1, BATCH), f32),
            pltpu.VMEM((1, BATCH), f32),
            pltpu.VMEM(obs_prior.shape, f32),
            pltpu.VMEM((1, BATCH), jnp.int32),
            pltpu.VMEM((8, HALF), f32),
            pltpu.VMEM((TILES, 8, HALF), f32),
            pltpu.VMEM((8, 8, HALF), f32),
            pltpu.VMEM((batches, 8, HALF), f32),
            pltpu.VMEM((8, 8, HALF), f32),
            pltpu.VMEM((8, batches - 1, 8, HALF), f32),
            pltpu.VMEM((batches, 8, HALF), f32),
            pltpu.VMEM((8, 8, 8, HALF), f32),
            pltpu.VMEM((8, 8, batches - 1, 8, HALF), f32),
            pltpu.VMEM(ensemble.shape, f32),
            pltpu.VMEM((8, rows, cells), bf16),
            pltpu.VMEM((8, rows, cells), bf16),
            pltpu.VMEM((8, rows, cells), bf16),
            pltpu.VMEM((MEMBERS, cells), f32),
            pltpu.VMEM((2 * batches, MEMBERS, BATCH), f32),
            pltpu.VMEM((batches, MEMBERS, BATCH), f32),
            pltpu.VMEM((2 * batches, 8, BATCH), f32),
            pltpu.VMEM((MEMBERS, HALF), f32),
            pltpu.VMEM((2, BATCH, 3 * MEMBERS), bf16),
            pltpu.VMEM((2, BATCH, 3 * MEMBERS), bf16),
            pltpu.VMEM((2, BATCH, HALF), f32),
            pltpu.VMEM((2, BATCH, HALF), f32),
            pltpu.VMEM((2, 3 * MEMBERS, BATCH), bf16),
            pltpu.VMEM((2, 3, BATCH, HALF), bf16),
            pltpu.VMEM((2, HALF, HALF), f32),
            pltpu.VMEM((2, 72 * HALF // 8, HALF), f32),
            pltpu.SemaphoreType.DMA((6,)),
            pltpu.SemaphoreType.DMA((11, 7)),
            pltpu.SemaphoreType.DMA((11, 7)),
        ],
        compiler_params=pltpu.CompilerParams(collective_id=0, has_side_effects=True, vmem_limit_bytes=63 << 20),
        name="regress_all",
    )(
        ensemble, obs_prior, obs_value[None], obs_var[None], obs_noise, obs_block[None], batch_owner
    )


def solution(mesh):
    return jax.shard_map(
        shards,
        mesh=mesh,
        in_specs=(
            P("mem", "col", None),
            P(None, "col"),
            P("col"),
            P("col"),
            P(None, "col"),
            P("col"),
            P(),
        ),
        out_specs=(P("mem", "col", None), P(None, "col")),
        check_vma=False,
    )
```

```python
import functools
import math

import jax
import jax.numpy as jnp
from jax import lax
from jax.experimental import pallas as pl
from jax.experimental.pallas import tpu as pltpu
from jax.sharding import PartitionSpec as P

MESH = pl.DeviceIdType.MESH
MEMBERS = 80
BATCH = 256
HALF = 128
GROUPS = 6
TILES = 8 * GROUPS
LEAD = 2


def split(x, n):
    parts = []
    for _ in range(n - 1):
        parts.append(x.astype(jnp.bfloat16))
        x = x - parts[-1].astype(jnp.float32)
    parts.append(x.astype(jnp.bfloat16))
    return parts


def once(a, b):
    return jnp.dot(a, b, preferred_element_type=jnp.float32)


def cat0(*v):
    return jnp.concatenate(v, 0)


def cat1(*v):
    return jnp.concatenate(v, 1)


def narrow(a, b):
    p, q = split(a, 3), split(b, 3)
    front = cat1(p[0], p[1])
    return (once(cat1(p[0], p[2]), cat0(q[2], q[0])) + once(front, cat0(q[1], q[1]))) + once(front, cat0(q[0], q[0]))


def wide_sum(stack, n, q):
    top = once(stack, q[0])
    middle = once(stack[: 2 * n], q[1])
    low = once(stack[:n], q[2])
    return top[:n] + ((top[n : 2 * n] + middle[:n]) + (top[2 * n :] + middle[n:] + low))


def eighth(x):
    x = x * x
    x = x * x
    return x * x


def lanes(x, j):
    return jnp.broadcast_to(x[:, j : j + 1], x.shape)


def pivot_rows(rows_in, columns, k, lane, board):
    for j in range(8):
        board[8 * j : 8 * j + 8, :] = columns[j]
    board[64:72, :] = rows_in
    a = {}
    for j in range(8):
        for i in range(j, 8):
            a[i, j] = jnp.broadcast_to(board[8 * j + i : 8 * j + i + 1, :], (8, HALF))
    rows = [jnp.broadcast_to(board[64 + i : 65 + i, :], (8, HALF)) for i in range(8)]
    for j in range(0, 8, 2):
        p, q, d = a[j, j], a[j + 1, j], a[j + 1, j + 1]
        r = 1.0 / (p * d - q * q)
        pi, qi, di = d * r, -(q * r), p * r
        m0 = lane == k + j
        m1 = lane == k + j + 1
        both = m0 | m1
        r0 = jnp.where(both, jnp.where(m0, 1.0, 0.0), rows[j])
        r1 = jnp.where(both, jnp.where(m1, 1.0, 0.0), rows[j + 1])
        w0 = pi * r0 + qi * r1
        w1 = qi * r0 + di * r1
        rows[j], rows[j + 1] = w0, w1
        for i in range(8):
            if i in (j, j + 1):
                continue
            if i > j:
                rows[i] = jnp.where(both, 0.0, rows[i]) - (a[i, j] * w0 + a[i, j + 1] * w1)
            else:
                rows[i] = jnp.where(both, 0.0, rows[i]) + (a[j, i] * w0 + a[j + 1, i] * w1)
        old = dict(a)
        for n in range(j + 2, 8):
            u0 = pi * old[n, j] + qi * old[n, j + 1]
            u1 = qi * old[n, j] + di * old[n, j + 1]
            for i in range(n, 8):
                a[i, n] = old[i, n] - (old[i, j] * u0 + old[i, j + 1] * u1)
            for i in range(0, j):
                a[n, i] = old[n, i] - (old[j, i] * u0 + old[j + 1, i] * u1)
            a[n, j], a[n, j + 1] = -u0, -u1
    return rows

def invert(a_ref, board, between):
    lane = lax.broadcasted_iota(jnp.int32, (8, HALF), 1)
    sub = lax.broadcasted_iota(jnp.int32, (8, HALF), 0)
    n = HALF // 8
    a = [a_ref[8 * v : 8 * v + 8, :] for v in range(n)]
    lower, scaled = [], []
    for block in range(n):
        k = 8 * block
        columns = {v: [lanes(a[v], k + j) for j in range(8)] for v in range(block, n)}
        rows = pivot_rows(a[block], columns[block], k, lane, board.at[pl.ds(72 * block, 72)])
        here = (lane >= k) & (lane < k + 8)
        w = rows[0]
        for i in range(1, 8):
            w = jnp.where(sub == i, rows[i], w)
        scaled.append(jnp.where(lane < k + 8, w, 0.0))
        lower.append(jnp.where(lane < k, a[block], jnp.where(lane == k + sub, 1.0, 0.0)))
        for v in range(block + 1, n):
            t = [columns[v][j] * rows[j] for j in range(8)]
            s = ((t[0] + t[1]) + (t[2] + t[3])) + ((t[4] + t[5]) + (t[6] + t[7]))
            a[v] = jnp.where(here, 0.0, a[v]) - s
        between()
    return narrow(jnp.concatenate(lower, 0).T, jnp.concatenate(scaled, 0))


class Regression:
    def __init__(self, p, turned, turned_low, cosine, sine, solved, gains):
        self.p = p
        self.turned, self.turned_low, self.cosine, self.sine = turned, turned_low, cosine, sine
        self.solved, self.gains = solved, gains

    def weight(self, c, s):
        return eighth(self.cosine[self.p] * c + self.sine[self.p] * s)

    def across(self, field):
        f = split(field, 3)
        total = once(self.turned_low[self.p], cat0(f[1], f[0], f[2])) + once(self.turned[self.p], cat0(f[0], f[0], f[1]))
        return total * (1.0 / (MEMBERS - 1))

    def gain(self, i, field, c, s):
        for q, part in enumerate(split(self.weight(c, s) * self.across(field), 3)):
            self.gains[i, q] = part

    def add(self, i, field):
        return field + wide_sum(self.solved[self.p], MEMBERS, [self.gains[i, q] for q in range(3)])


def later(regression, fields):
    for i, (read, write, c, s) in enumerate(fields):
        regression.gain(i % 2, read(), c(), s())
        yield
        write(regression.add(i % 2, read()))
        yield


def columns_of(ref, k, facts):
    for t in range(2):
        part = slice(t * HALF, t * HALF + HALF)

        def write(value, part=part):
            ref[k, :, part] = value

        yield (
            lambda part=part: ref[k, :, part],
            write,
            lambda part=part: facts[k, 1:2, part],
            lambda part=part: facts[k, 2:3, part],
        )


def assimilate(batches, pool, target, facts, carry, blockrow, turned, turned_low, cosine, sine, solved, gains, half, board, hooks):
    own = pool.shape[0] - 1
    turned[1] = jnp.zeros(turned.shape[1:], turned.dtype)
    turned_low[1] = jnp.zeros(turned.shape[1:], turned.dtype)
    cosine[1] = jnp.zeros(cosine.shape[1:], jnp.float32)
    sine[1] = jnp.zeros(cosine.shape[1:], jnp.float32)
    solved[1] = jnp.zeros(solved.shape[1:], solved.dtype)
    row = lax.broadcasted_iota(jnp.int32, carry.shape, 0)
    carry[...] = jnp.where(row == lax.broadcasted_iota(jnp.int32, carry.shape, 1), 1.0, 0.0)

    def keep(value):
        carry[...] = value

    mine = list(columns_of(pool, own, facts)) + [
        (lambda: carry[...], keep, lambda: blockrow[0:1, :], lambda: blockrow[1:2, :])
    ]
    factors = (turned, turned_low, cosine, sine, solved, gains)

    @pl.loop(0, batches)
    def _(b):
        now = lax.rem(b, 2)
        here = Regression(now, *factors)
        before = Regression(1 - now, *factors)
        priors = pool[b]
        spread = priors - jnp.sum(priors, axis=0, keepdims=True) * (1.0 / MEMBERS)
        s0, s1, s2 = split(spread, 3)
        turned[now] = cat0(s0, s1, s0).T
        turned_low[now] = cat0(s1, s2, s0).T
        gap = target[b] - priors
        fact = facts[b]
        var, cos, sin = fact[0:1], fact[1:2], fact[2:3]
        cosine[now] = jnp.broadcast_to(cos, (HALF, BATCH)).T
        sine[now] = jnp.broadcast_to(sin, (HALF, BATCH)).T
        row = lax.broadcasted_iota(jnp.int32, (BATCH, HALF), 0)
        lane = lax.broadcasted_iota(jnp.int32, (BATCH, HALF), 1)
        covariance = here.across(spread)

        def system(t):
            part = slice(t * HALF, t * HALF + HALF)
            w = here.weight(cos[:, part], sin[:, part])
            return w * covariance[:, part] + jnp.where(row == lane + t * HALF, var[:, part], 0.0)

        left, right = system(0), system(1)
        a12 = right[:HALF]
        half[0] = left[:HALF]
        hooks[0](b)
        fields = list(mine)
        for i in range(batches - 2):
            fields += columns_of(pool, b + 2 - 1 + i, facts)
        steps = later(before, fields)
        done = object()
        between = lambda: next(steps, done)
        first = invert(half.at[0], board.at[0], between)
        both = narrow(cat0(left[HALF:], gap[:, :HALF]), first)
        schur = cat0(right[HALF:], gap[:, HALF:]) - narrow(both, a12)
        half[1] = schur[:HALF]
        hooks[1](b)
        second = invert(half.at[1], board.at[1], between)
        for _ in steps:
            pass
        x2 = narrow(schur[HALF:], second)
        x1 = both[HALF:] - narrow(x2, both[:HALF])
        solved[now] = cat0(*split(cat1(x1, x2), 3))
        hooks[2](b)
        for _ in later(here, columns_of(pool, b + 1, facts)):
            pass

    return Regression((batches - 1) % 2, *factors), mine


def regress_all(
    ens_hbm, prior_hbm, value_hbm, var_hbm, noise_hbm, place_hbm, owner_ref,
    out_ref, post_ref,
    ens, prior, value, var_in, noise, place, blockrow,
    tiles, along_y, picked, along_z, along_z_rest, chosen, every, every_rest, wide, going, coming, back,
    state, pool, target, facts, carry, turned, turned_low, cosine, sine, solved, gains, half, board,
    loads, sends, recvs,
):
    m = lax.axis_index("mem")
    c = lax.axis_index("col")
    x, core = m // 2, lax.rem(m, 2)
    z, y = c // 8, lax.rem(c, 8)
    batches = target.shape[0]
    own = pool.shape[0] - 1
    rows, blocks_own, _ = ens.shape
    step = math.pi / (blocks_own * lax.axis_size("col"))
    arrived = [
        pltpu.make_async_copy(far, near, loads.at[i])
        for i, (far, near) in enumerate(
            [
                (value_hbm, value),
                (var_hbm, var_in),
                (place_hbm, place),
                (prior_hbm, prior),
                (noise_hbm, noise),
                (ens_hbm, ens),
            ]
        )
    ]
    for load in arrived:
        load.start()
    to_y = [(m, z * 8 + lax.rem(y + i, 8)) for i in range(1, 8)]
    to_z = [(m, lax.rem(z + i, 8) * 8 + y) for i in range(1, 8)]
    to_m = [(lax.rem(m + i, 8), c) for i in range(1, 8)]
    to_x = [(lax.rem(x + i, 4) * 2 + core, c) for i in range(1, 4)]
    there = (x * 2 + 1 - core, c)
    barrier = pltpu.get_barrier_semaphore()
    for peer in to_y + to_z + to_m:
        pl.semaphore_signal(barrier, inc=1, device_id=peer, device_id_type=MESH)

    here = jnp.full((8, HALF), (c * blocks_own + m).astype(jnp.float32) * step)
    blockrow[...] = jnp.where(lax.broadcasted_iota(jnp.int32, (8, HALF), 0) == 0, jnp.cos(here), jnp.sin(here))
    for t in range(42, TILES):
        tiles[t] = jnp.zeros((8, HALF), jnp.float32)
    for load in arrived[:5]:
        load.wait()
    angle = place[...].astype(jnp.float32) * step
    cos, sin = jnp.cos(angle), jnp.sin(angle)
    perturbed = value[...] + jnp.sqrt(var_in[...]) * noise[...]
    for g in range(10):
        for t in range(2):
            lane = slice(t * HALF, t * HALF + HALF)
            tiles[2 * g + t] = prior[8 * g : 8 * g + 8, lane]
            tiles[20 + 2 * g + t] = perturbed[8 * g : 8 * g + 8, lane]
    fact = jnp.concatenate([var_in[...], cos, sin, jnp.zeros((5, BATCH), jnp.float32)], 0)
    for t in range(2):
        tiles[40 + t] = fact[:, t * HALF : t * HALF + HALF]
    pl.semaphore_wait(barrier, 21)

    def copy(phase, i, src, dst, peer):
        return pltpu.make_async_remote_copy(
            src_ref=src,
            dst_ref=dst,
            send_sem=sends.at[phase, i],
            recv_sem=recvs.at[phase, i],
            device_id=peer,
            device_id_type=MESH,
        )

    piece = lambda k: tiles.at[m * GROUPS + jnp.minimum(k, GROUPS - 1)]
    for i, peer in enumerate(to_y):
        copy(0, i, piece(lax.rem(y + i + 1, 8)), along_y.at[y], peer).start()
    along_y[y] = tiles[m * GROUPS + jnp.minimum(y, GROUPS - 1)]

    arrived[5].wait()
    wide[...] = ens[...].astype(jnp.float32)
    for g in range(8):
        going[g] = wide[:, g, :].astype(jnp.bfloat16)

    for b in range(batches, own):
        pool[b] = jnp.zeros(pool.shape[1:], jnp.float32)
        facts[b] = jnp.zeros(facts.shape[1:], jnp.float32)
    pool[own] = prior[...]
    facts[own] = fact

    def wait_recv(phase, i, src, dst, peer):
        copy(phase, i, src, dst, peer).wait_recv()

    for i, peer in enumerate(to_y):
        wait_recv(0, i, tiles.at[0], along_y.at[lax.rem(y + 7 - i, 8)], peer)
    owners = [owner_ref[j] for j in range(batches)]
    for j in range(batches):
        picked[j] = along_y[lax.rem(owners[j], 8)]
    lead, rest = pl.ds(0, LEAD), pl.ds(LEAD, batches - LEAD)
    for i, peer in enumerate(to_z):
        copy(1, i, picked.at[lead], along_z.at[z], peer).start()
    for i, peer in enumerate(to_z):
        copy(2, i, picked.at[rest], along_z_rest.at[z], peer).start()
    along_z[z] = picked[:LEAD]
    along_z_rest[z] = picked[LEAD:]
    for i, peer in enumerate(to_z):
        wait_recv(1, i, picked.at[lead], along_z.at[lax.rem(z + 7 - i, 8)], peer)
    for j in range(LEAD):
        chosen[j] = along_z[owners[j] // 8, j]
    for i, peer in enumerate(to_y):
        copy(3, i, chosen.at[lead], every.at[m, y], peer).start()
    every[m, y] = chosen[:LEAD]
    for i, peer in enumerate(to_y):
        wait_recv(3, i, chosen.at[lead], every.at[m, lax.rem(y + 7 - i, 8)], peer)
    used = pl.ds(0, GROUPS)
    mine = every.at[m, used]
    for i, peer in enumerate(to_x):
        copy(4, i, mine, mine, peer).start()
    copy(5, 0, mine, mine, there).start()

    def source(i):
        return lax.rem(x + 3 - i, 4) * 2

    for i, peer in enumerate(to_x):
        got = every.at[source(i) + core, used]
        wait_recv(4, i, got, got, peer)
        copy(5, i + 1, got, got, there).start()
    for i, peer in enumerate(to_m):
        copy(9, i, going.at[lax.rem(m + i + 1, 8)], coming.at[m], peer).start()
    coming[m] = going[m]
    wait_recv(5, 0, mine, every.at[there[0], used], there)
    for i, peer in enumerate(to_x):
        got = every.at[source(i) + 1 - core, used]
        wait_recv(5, i + 1, got, got, there)

    def unpack(get, b):
        for t in range(40):
            g, lane = t % 20 // 2, slice(t % 2 * HALF, t % 2 * HALF + HALF)
            to = pool if t < 20 else target
            to[b, 8 * g : 8 * g + 8, lane] = get(t // GROUPS, t % GROUPS)
        for t in range(40, 42):
            lane = slice(t % 2 * HALF, t % 2 * HALF + HALF)
            facts[b, :, lane] = get(t // GROUPS, t % GROUPS)

    for j in range(LEAD):
        unpack(lambda p, q: every[p, q, j], j)
    def pick_rest(b):
        @pl.when(b == 0)
        def _():
            for i, peer in enumerate(to_z):
                wait_recv(2, i, picked.at[rest], along_z_rest.at[lax.rem(z + 7 - i, 8)], peer)
            for j in range(LEAD, batches):
                chosen[j] = along_z_rest[owners[j] // 8, j - LEAD]
            for i, peer in enumerate(to_y):
                copy(6, i, chosen.at[rest], every_rest.at[m, y], peer).start()
            every_rest[m, y] = chosen[LEAD:]

    def spread_rest(b):
        @pl.when(b == 0)
        def _():
            for i, peer in enumerate(to_y):
                wait_recv(6, i, chosen.at[rest], every_rest.at[m, lax.rem(y + 7 - i, 8)], peer)
            part = every_rest.at[m, used]
            for i, peer in enumerate(to_x):
                copy(7, i, part, part, peer).start()
            copy(8, 0, part, part, there).start()

    def forward_rest(b):
        @pl.when(b == 0)
        def _():
            for i, peer in enumerate(to_x):
                got = every_rest.at[source(i) + core, used]
                wait_recv(7, i, got, got, peer)
                copy(8, i + 1, got, got, there).start()

    def take_rest(b):
        @pl.when(b == LEAD - 1)
        def _():
            wait_recv(8, 0, every_rest.at[m, used], every_rest.at[there[0], used], there)
            for i, peer in enumerate(to_x):
                got = every_rest.at[source(i) + 1 - core, used]
                wait_recv(8, i + 1, got, got, there)

            @pl.loop(LEAD, batches)
            def _(k):
                unpack(lambda p, q: every_rest[p, q, k - LEAD], k)

            for i, peer in enumerate(to_m):
                wait_recv(9, i, going.at[0], coming.at[lax.rem(m + 7 - i, 8)], peer)
            for g in range(8):
                state[rows * g : rows * g + rows, :] = coming[g].astype(jnp.float32)

    last, fields = assimilate(
        batches, pool, target, facts, carry, blockrow, turned, turned_low, cosine, sine, solved, gains, half, board,
        (lambda b: (pick_rest(b), take_rest(b)), spread_rest, forward_rest),
    )

    for i, peer in enumerate(to_y):
        copy(0, i, tiles.at[0], along_y.at[y], peer).wait_send()
        copy(3, i, chosen.at[lead], every.at[m, y], peer).wait_send()
        copy(6, i, chosen.at[rest], every_rest.at[m, y], peer).wait_send()
    for i, peer in enumerate(to_z):
        copy(1, i, picked.at[lead], along_z.at[z], peer).wait_send()
        copy(2, i, picked.at[rest], along_z_rest.at[z], peer).wait_send()
    part = every_rest.at[m, used]
    for i, peer in enumerate(to_x):
        copy(4, i, mine, mine, peer).wait_send()
        copy(7, i, part, part, peer).wait_send()
    for i in range(4):
        copy(5, i, mine, mine, there).wait_send()
        copy(8, i, part, part, there).wait_send()
    for i, peer in enumerate(to_m):
        copy(9, i, going.at[0], coming.at[m], peer).wait_send()

    for _ in later(last, fields[2:]):
        pass
    final = cat1(*split(carry[...][:, :MEMBERS], 3))
    for t in range(0, state.shape[1], BATCH):
        part = slice(t, t + BATCH)
        f = state[:, part].astype(jnp.bfloat16)
        state[:, part] = once(final, cat0(f, f, f))
    for g in range(8):
        going[g] = state[rows * g : rows * g + rows, :].astype(jnp.bfloat16)
    for i, peer in enumerate(to_m):
        copy(10, i, going.at[lax.rem(m + i + 1, 8)], back.at[m], peer).start()
    back[m] = going[m]
    for _ in later(last, fields[:2]):
        pass
    post_ref[...] = pool[own]
    for i, peer in enumerate(to_m):
        one = copy(10, i, going.at[0], back.at[lax.rem(m + 7 - i, 8)], peer)
        one.wait_recv()
        one.wait_send()
    for g in range(8):
        wide[:, g, :] = back[g].astype(jnp.float32)
    out_ref[...] = wide[...].astype(jnp.bfloat16)


def shards(ensemble, obs_prior, obs_value, obs_var, obs_noise, obs_block, batch_owner):
    rows, _, cells = ensemble.shape
    batches = batch_owner.shape[0]
    vmem = pl.BlockSpec(memory_space=pltpu.VMEM)
    f32, bf16 = jnp.float32, jnp.bfloat16
    return pl.pallas_call(
        regress_all,
        out_shape=(
            jax.ShapeDtypeStruct(ensemble.shape, bf16),
            jax.ShapeDtypeStruct(obs_prior.shape, f32),
        ),
        in_specs=[pl.BlockSpec(memory_space=pltpu.HBM)] * 6 + [pl.BlockSpec(memory_space=pltpu.SMEM)],
        out_specs=(vmem, vmem),
        scratch_shapes=[
            pltpu.VMEM(ensemble.shape, bf16),
            pltpu.VMEM(obs_prior.shape, f32),
            pltpu.VMEM((1, BATCH), f32),
            pltpu.VMEM((1, BATCH), f32),
            pltpu.VMEM(obs_prior.shape, f32),
            pltpu.VMEM((1, BATCH), jnp.int32),
            pltpu.VMEM((8, HALF), f32),
            pltpu.VMEM((TILES, 8, HALF), f32),
            pltpu.VMEM((8, 8, HALF), f32),
            pltpu.VMEM((batches, 8, HALF), f32),
            pltpu.VMEM((8, LEAD, 8, HALF), f32),
            pltpu.VMEM((8, batches - LEAD, 8, HALF), f32),
            pltpu.VMEM((batches, 8, HALF), f32),
            pltpu.VMEM((8, 8, LEAD, 8, HALF), f32),
            pltpu.VMEM((8, 8, batches - LEAD, 8, HALF), f32),
            pltpu.VMEM(ensemble.shape, f32),
            pltpu.VMEM((8, rows, cells), bf16),
            pltpu.VMEM((8, rows, cells), bf16),
            pltpu.VMEM((8, rows, cells), bf16),
            pltpu.VMEM((MEMBERS, cells), f32),
            pltpu.VMEM((2 * batches, MEMBERS, BATCH), f32),
            pltpu.VMEM((batches, MEMBERS, BATCH), f32),
            pltpu.VMEM((2 * batches, 8, BATCH), f32),
            pltpu.VMEM((MEMBERS, HALF), f32),
            pltpu.VMEM((2, BATCH, 3 * MEMBERS), bf16),
            pltpu.VMEM((2, BATCH, 3 * MEMBERS), bf16),
            pltpu.VMEM((2, BATCH, HALF), f32),
            pltpu.VMEM((2, BATCH, HALF), f32),
            pltpu.VMEM((2, 3 * MEMBERS, BATCH), bf16),
            pltpu.VMEM((2, 3, BATCH, HALF), bf16),
            pltpu.VMEM((2, HALF, HALF), f32),
            pltpu.VMEM((2, 72 * HALF // 8, HALF), f32),
            pltpu.SemaphoreType.DMA((6,)),
            pltpu.SemaphoreType.DMA((11, 7)),
            pltpu.SemaphoreType.DMA((11, 7)),
        ],
        compiler_params=pltpu.CompilerParams(collective_id=0, has_side_effects=True, vmem_limit_bytes=63 << 20),
        name="regress_all",
    )(
        ensemble, obs_prior, obs_value[None], obs_var[None], obs_noise, obs_block[None], batch_owner
    )


def solution(mesh):
    return jax.shard_map(
        shards,
        mesh=mesh,
        in_specs=(
            P("mem", "col", None),
            P(None, "col"),
            P("col"),
            P("col"),
            P(None, "col"),
            P("col"),
            P(),
        ),
        out_specs=(P("mem", "col", None), P(None, "col")),
        check_vma=False,
    )
```
